32 devices in a mesh: dp: 8 (over z, y), pipe: 4 (over x, core).
Axes of the slice: x: 2, y: 2, z: 4, core: 2. Of those that a mesh axis runs over, the one named last changes fastest.
Arguments:
- series_input: float32 [2, 180, 256, 128], P(None, None, 'dp'), may hold values from -6 to 6
- cotangent: float32 [2, 180, 256, 128], P(None, None, 'dp'), may hold values from -6 to 6
- season_enter_first: bfloat16 [2, 48, 96], replicated, may hold values from -0.625 to 0.625
- season_enter_second: bfloat16 [2, 24, 48], replicated, may hold values from -0.875 to 0.875
- season_enter_third: bfloat16 [2, 12, 24], replicated, may hold values from -1.25 to 1.25
- season_leave_first: bfloat16 [2, 48, 48], replicated, may hold values from -0.875 to 0.875
- season_leave_second: bfloat16 [2, 24, 24], replicated, may hold values from -1.25 to 1.25
- season_leave_third: bfloat16 [2, 12, 12], replicated, may hold values from -1.75 to 1.75
- season_bias: bfloat16 [2, 2, 84], replicated, may hold values from -3 to 3
- trend_enter_first: bfloat16 [2, 96, 48], replicated, may hold values from -0.875 to 0.875
- trend_enter_second: bfloat16 [2, 48, 24], replicated, may hold values from -1.25 to 1.25
- trend_enter_third: bfloat16 [2, 24, 12], replicated, may hold values from -1.75 to 1.75
- trend_leave_first: bfloat16 [2, 96, 96], replicated, may hold values from -0.625 to 0.625
- trend_leave_second: bfloat16 [2, 48, 48], replicated, may hold values from -0.875 to 0.875
- trend_leave_third: bfloat16 [2, 24, 24], replicated, may hold values from -1.25 to 1.25
- trend_bias: bfloat16 [2, 2, 168], replicated, may hold values from -3 to 3
- expand_weight: bfloat16 [2, 128, 256], replicated, may hold values from -0.5 to 0.5
- expand_bias: bfloat16 [2, 256], replicated, may hold values from -3 to 3
- shrink_weight: bfloat16 [2, 256, 128], replicated, may hold values from -0.375 to 0.375
- shrink_bias: bfloat16 [2, 128], replicated, may hold values from -3 to 3
- norm_gain: bfloat16 [2, 4, 128], replicated, may hold values from 0.5 to 1.5
- norm_shift: bfloat16 [2, 4, 128], replicated, may hold values from -3 to 3
Outputs:
- layer_output: float32 [2, 180, 256, 128], P(None, None, 'dp')
- input_grad: float32 [2, 180, 256, 128], P(None, None, 'dp')
- grad_season_enter_first: float32 [2, 48, 96], replicated
- grad_season_enter_second: float32 [2, 24, 48], replicated
- grad_season_enter_third: float32 [2, 12, 24], replicated
- grad_season_leave_first: float32 [2, 48, 48], replicated
- grad_season_leave_second: float32 [2, 24, 24], replicated
- grad_season_leave_third: float32 [2, 12, 12], replicated
- grad_season_bias: float32 [2, 2, 84], replicated
- grad_trend_enter_first: float32 [2, 96, 48], replicated
- grad_trend_enter_second: float32 [2, 48, 24], replicated
- grad_trend_enter_third: float32 [2, 24, 12], replicated
- grad_trend_leave_first: float32 [2, 96, 96], replicated
- grad_trend_leave_second: float32 [2, 48, 48], replicated
- grad_trend_leave_third: float32 [2, 24, 24], replicated
- grad_trend_bias: float32 [2, 2, 168], replicated
- grad_expand_weight: float32 [2, 128, 256], replicated
- grad_expand_bias: float32 [2, 256], replicated
- grad_shrink_weight: float32 [2, 256, 128], replicated
- grad_shrink_bias: float32 [2, 128], replicated
- grad_norm_gain: float32 [2, 4, 128], replicated
- grad_norm_shift: float32 [2, 4, 128], replicated
The draws below stay inside these ranges and needn't reach their ends.
All inputs are finite; a program needn't handle non-finite values.
Results may differ from the reference program's by a relative error of at most 0.022.
Values may be sent and summed in bfloat16 or wider, within the bound.
No kernel may reach another device: no remote copies, remote signals or barrier semaphores. Data moves between devices by JAX's collectives and lax.ppermute only.
A program may use at most 192 MiB of HBM per device.

```python
import jax
import jax.numpy as jnp
from jax import lax

D = 128
FF = 256
L0 = 96
KERNEL = 25
LAYERS = 2
MICRO = 2
L1 = 48
L2 = 24
L3 = 12
TT = 180
SERIES = 256


def block_scale(key, dims, split, smallest, largest):
    gain = 1.0
    for position, blocks in split:
        steps = jax.random.uniform(jax.random.fold_in(jax.random.fold_in(key, 6), position), (blocks,), jnp.float32, smallest / len(split), largest / len(split))
        gain = gain * jnp.repeat(jnp.exp(steps), dims[position] // blocks).reshape((-1,) + (1,) * (len(dims) - 1 - position))
    return gain


def normal_values(own_key, extent, scale, most, cuts=(), kind=jnp.bfloat16):
    entries = scale * jax.random.normal(own_key, extent, jnp.float32)
    if cuts:
        entries = entries * block_scale(own_key, extent, cuts, -0.22, 0.18)
    return jnp.clip(entries, -most, most).astype(kind)


def setup_inputs(seed: int = 0) -> dict:
    key_of = jax.random.split(jax.random.key(seed), 23)
    return {
        "series_input": normal_values(key_of[0], (MICRO, TT, SERIES, D), 1.0, 6.0, ((2, 8),), jnp.float32),
        "cotangent": normal_values(key_of[1], (MICRO, TT, SERIES, D), 1.0, 6.0, ((2, 8),), jnp.float32),
        "season_enter_first": normal_values(key_of[2], (LAYERS, L1, L0), L0 ** -0.5, 0.625),
        "season_enter_second": normal_values(key_of[3], (LAYERS, L2, L1), L1 ** -0.5, 0.875),
        "season_enter_third": normal_values(key_of[4], (LAYERS, L3, L2), L2 ** -0.5, 1.25),
        "season_leave_first": normal_values(key_of[5], (LAYERS, L1, L1), L1 ** -0.5, 0.875),
        "season_leave_second": normal_values(key_of[6], (LAYERS, L2, L2), L2 ** -0.5, 1.25),
        "season_leave_third": normal_values(key_of[7], (LAYERS, L3, L3), L3 ** -0.5, 1.75),
        "season_bias": normal_values(key_of[8], (LAYERS, 2, L1 + L2 + L3), 0.5, 3.0),
        "trend_enter_first": normal_values(key_of[9], (LAYERS, L0, L1), L1 ** -0.5, 0.875),
        "trend_enter_second": normal_values(key_of[10], (LAYERS, L1, L2), L2 ** -0.5, 1.25),
        "trend_enter_third": normal_values(key_of[11], (LAYERS, L2, L3), L3 ** -0.5, 1.75),
        "trend_leave_first": normal_values(key_of[12], (LAYERS, L0, L0), L0 ** -0.5, 0.625),
        "trend_leave_second": normal_values(key_of[13], (LAYERS, L1, L1), L1 ** -0.5, 0.875),
        "trend_leave_third": normal_values(key_of[14], (LAYERS, L2, L2), L2 ** -0.5, 1.25),
        "trend_bias": normal_values(key_of[15], (LAYERS, 2, L0 + L1 + L2), 0.5, 3.0),
        "expand_weight": normal_values(key_of[16], (LAYERS, D, FF), D ** -0.5, 0.5),
        "expand_bias": normal_values(key_of[17], (LAYERS, FF), 0.5, 3.0),
        "shrink_weight": normal_values(key_of[18], (LAYERS, FF, D), FF ** -0.5, 0.375),
        "shrink_bias": normal_values(key_of[19], (LAYERS, D), 0.5, 3.0),
        "norm_gain": jnp.clip(jax.random.uniform(key_of[20], (LAYERS, 4, D), jnp.float32, 0.5, 1.5), 0.5, 1.5).astype(jnp.bfloat16),
        "norm_shift": normal_values(key_of[21], (LAYERS, 4, D), 0.5, 3.0),
    }


EPSILON = 1e-05
PRECISE = lax.Precision.HIGHEST

@jax.custom_vjp
def low(v):
    return lax.optimization_barrier(v.astype(jnp.bfloat16)).astype(jnp.float32)

@jax.custom_vjp
def low_back(v):
    return v

def low_keep(v):
    return (low(v), None)

def low_pass(kept, grad):
    return (grad,)

def back_keep(v):
    return (v, None)

def back_low(kept, grad):
    return (low(grad),)
low.defvjp(low_keep, low_pass)
low_back.defvjp(back_keep, back_low)

def average_matrix(length):
    row_index = jnp.arange(length)[:, None]
    reached = jnp.clip(row_index + jnp.arange(KERNEL)[None, :] - KERNEL // 2, 0, length - 1)
    matches = (reached[:, :, None] == jnp.arange(length)[None, None, :]).astype(jnp.float32)
    return lax.optimization_barrier(jnp.sum(matches, axis=1)) / KERNEL

def scale_layout():
    lengths = [L0 // 2 ** scale_at for scale_at in range(4)]
    starts = [sum(lengths[:scale_at]) for scale_at in range(4)]
    return (lengths, starts)

def normalize(residual, gain_row, shift_row):
    average = lax.optimization_barrier(jnp.mean(residual, axis=-1, keepdims=True))
    centred = residual - average
    spread = lax.optimization_barrier(jnp.mean(centred * centred, axis=-1, keepdims=True))
    return centred * lax.rsqrt(spread + EPSILON) * gain_row + shift_row

def time_mix(source, enter_weight, enter_bias, leave_weight, leave_bias):
    before = low_back(jnp.dot(enter_weight, low(source), precision=PRECISE) + enter_bias[:, None])
    return low_back(jnp.dot(leave_weight, low(jax.nn.gelu(before)), precision=PRECISE) + leave_bias[:, None])

def layer(block_in, weights):
    lengths, starts = scale_layout()
    season_enter = weights[0:3]
    season_leave = weights[3:6]
    season_bias = weights[6]
    trend_enter = weights[7:10]
    trend_leave = weights[10:13]
    trend_bias = weights[13]
    expand_weight, expand_bias, shrink_weight, shrink_bias, norm_gain, norm_shift = weights[14:20]
    pieces = [block_in[starts[scale_at]:starts[scale_at] + lengths[scale_at]] for scale_at in range(4)]
    trends = [jnp.dot(average_matrix(lengths[scale_at]), pieces[scale_at], precision=PRECISE) for scale_at in range(4)]
    seasons = [pieces[scale_at] - trends[scale_at] for scale_at in range(4)]
    mixed_season = [seasons[0]]
    for scale_at in range(3):
        offset = starts[scale_at + 1] - lengths[0]
        span_len = lengths[scale_at + 1]
        mixed_in = time_mix(mixed_season[scale_at], season_enter[scale_at], season_bias[0, offset:offset + span_len], season_leave[scale_at], season_bias[1, offset:offset + span_len])
        mixed_season.append(seasons[scale_at + 1] + mixed_in)
    mixed_trend = [None, None, None, trends[3]]
    for scale_at in (2, 1, 0):
        offset = starts[scale_at]
        span_len = lengths[scale_at]
        mixed_in = time_mix(mixed_trend[scale_at + 1], trend_enter[scale_at], trend_bias[0, offset:offset + span_len], trend_leave[scale_at], trend_bias[1, offset:offset + span_len])
        mixed_trend[scale_at] = trends[scale_at] + mixed_in
    outputs = []
    for scale_at in range(4):
        joined = low(mixed_season[scale_at] + mixed_trend[scale_at]).reshape(-1, D)
        hidden = low_back(jnp.dot(joined, expand_weight, precision=PRECISE) + expand_bias)
        branch = low_back(jnp.dot(low(jax.nn.gelu(hidden)), shrink_weight, precision=PRECISE) + shrink_bias)
        residual = pieces[scale_at].reshape(-1, D) + branch
        normed = normalize(residual, norm_gain[scale_at], norm_shift[scale_at])
        outputs.append(normed.reshape(lengths[scale_at], -1))
    return jnp.concatenate(outputs, axis=0)

def reference(series_input, cotangent, season_enter_first, season_enter_second, season_enter_third, season_leave_first, season_leave_second, season_leave_third, season_bias, trend_enter_first, trend_enter_second, trend_enter_third, trend_leave_first, trend_leave_second, trend_leave_third, trend_bias, expand_weight, expand_bias, shrink_weight, shrink_bias, norm_gain, norm_shift):
    weights = tuple((weight_in.astype(jnp.float32) for weight_in in (season_enter_first, season_enter_second, season_enter_third, season_leave_first, season_leave_second, season_leave_third, season_bias, trend_enter_first, trend_enter_second, trend_enter_third, trend_leave_first, trend_leave_second, trend_leave_third, trend_bias, expand_weight, expand_bias, shrink_weight, shrink_bias, norm_gain, norm_shift)))

    def both_layers(inputs, params):
        flat = inputs.reshape(inputs.shape[0], -1)
        hidden = low_back(low(layer(flat, tuple((param[0] for param in params)))))
        return layer(hidden, tuple((param[1] for param in params))).reshape(inputs.shape)

    def one_micro(running, block_in):
        inputs, tangent = block_in
        result, pull = jax.vjp(both_layers, inputs, weights)
        back_input, back_weights = pull(tangent)
        running = tuple((so_far + extra for so_far, extra in zip(running, back_weights)))
        return (running, (result, back_input))
    initial = tuple((jnp.zeros(weight_in.shape, jnp.float32) for weight_in in weights))
    totals, (outputs, backs) = lax.scan(one_micro, initial, (series_input, cotangent))
    return (outputs, backs, totals[0], totals[1], totals[2], totals[3], totals[4], totals[5], totals[6], totals[7], totals[8], totals[9], totals[10], totals[11], totals[12], totals[13], totals[14], totals[15], totals[16], totals[17], totals[18], totals[19])
```

```python
import functools

import jax
import jax.numpy as jnp
import numpy as np
from jax import lax
from jax.experimental import pallas as pl
from jax.experimental.pallas import tpu as pltpu
from jax.sharding import PartitionSpec as P

F32 = jnp.float32
BF16 = jnp.bfloat16

LENGTHS = (96, 48, 24, 12)
STARTS = (0, 96, 144, 168)
STEPS = 180
ROWS = 192
KERNEL = 25
LAYERS = 2
WIDTH = 128
HIDDEN = 256
GROUP = 8
EPSILON = 1e-05

ROWS_OF = {96: 96, 48: 48, 24: 24, 12: 16}
AUG = {96: 112, 48: 64, 24: 32, 12: 16}
DEEP = {96: 96, 48: 48, 24: 32, 12: 16}

FROM = (96, 48, 24, 12, 24, 48)
TO = (48, 24, 12, 24, 48, 96)
BIAS_AT = (0, 48, 72, 144, 96, 0)
ENTER_ARG = (0, 1, 2, 9, 8, 7)
LEAVE_ARG = (3, 4, 5, 12, 11, 10)
BIAS_ARG = (6, 6, 6, 13, 13, 13)

ORDER = {2: (1, 0, 2), 5: (1, 0, 2), 7: (0, 2, 1), 8: (0, 2, 1), 9: (2, 0, 1)}
MIDDLE = (2, 5, 9)
TURNED = (7, 8, 9)


def offsets(sizes):
    total, found = 0, []
    for size in sizes:
        found.append(total)
        total += size
    return found, total


SOURCE_AT, SOURCE_ROWS = offsets([AUG[n] for n in FROM])
ACTIVE_AT, ACTIVE_ROWS = offsets([AUG[n] for n in TO])
SLOPE_AT, SLOPE_ROWS = offsets([ROWS_OF[n] for n in TO])
FROM_AT, FROM_ROWS = offsets([DEEP[n] for n in FROM])
TO_AT, TO_ROWS = offsets([DEEP[n] for n in TO])

PIECES = ((0, 48, 0), (48, 96, 0), (96, 144, 1), (144, 168, 2), (168, 192, 3))

VECTORS_AT = 288
EXPAND_AT = 304
SHRINK_AT = 560
USED_ROWS = 816

GELU_A = 0.7978845608028654
GELU_B = GELU_A * 0.044715


def dot(left, right):
    return lax.dot_general(left, right, (((1,), (0,)), ((), ())), preferred_element_type=F32)


def dot_last(left, right):
    return lax.dot_general(left, right, (((1,), (1,)), ((), ())), preferred_element_type=F32)


def dot_first(left, right):
    return lax.dot_general(left, right, (((0,), (0,)), ((), ())), preferred_element_type=F32)


def gelu_and_slope(u):
    square = u * u
    half = jnp.tanh(u * (GELU_A + GELU_B * square)) * 0.5 + 0.5
    value = u * half
    slope = half + (value - value * half) * (2.0 * GELU_A + 6.0 * GELU_B * square)
    return value, slope


def iota(shape, dim):
    return lax.broadcasted_iota(jnp.int32, shape, dim)


def eye(rows, lanes):
    return (iota((rows, lanes), 0) == iota((rows, lanes), 1)).astype(F32)


def moving_average():
    total = np.zeros((ROWS, ROWS), np.float32)
    for start, length in zip(STARTS, LENGTHS):
        for row in range(length):
            for offset in range(KERNEL):
                reached = min(max(row + offset - KERNEL // 2, 0), length - 1)
                total[start + row, start + reached] += 1.0
    return total


def prepare(weights, keep):
    keep.means[...] = keep.counts[...].astype(BF16)
    keep.stage[...] = jnp.zeros(keep.stage.shape, F32)
    unit = eye(WIDTH, WIDTH).astype(BF16)
    for layer in range(LAYERS):
        for block in range(6):
            rows, cols = TO[block], FROM[block]
            full = DEEP[rows]
            enter_back = keep.enter_back.at[layer, FROM_AT[block] : FROM_AT[block] + DEEP[cols]]
            near = slice(TO_AT[block], TO_AT[block] + full)
            leave_back = keep.leave_back.at[layer, near]
            for arg, depth, place, straight, back in (
                (ENTER_ARG[block], cols, 0, keep.enter.at[layer, near], enter_back),
                (LEAVE_ARG[block], rows, 1, keep.leave.at[layer, near], leave_back),
            ):
                stage = keep.stage.at[layer, block, place]
                if arg in MIDDLE:
                    value = weights[arg][...].astype(F32)[:, layer, :]
                else:
                    value = weights[arg][layer].astype(F32)
                stage[0 : value.shape[0], 0 : value.shape[1]] = value
                if arg in TURNED:
                    turned = dot_last(unit, stage[...].astype(BF16))
                    stage[:, 0:96] = turned[0:96]
                    stage[:, 96:] = jnp.zeros((96, WIDTH - 96), F32)
                matrix = stage[0:full, :]
                source = weights[BIAS_ARG[block]][layer, place : place + 1, :].astype(F32)
                at = BIAS_AT[block]
                lanes = source.shape[1]
                pick = iota((full, lanes), 1) - at == iota((full, lanes), 0)
                pick = pick & (iota((full, lanes), 0) < rows)
                column = jnp.sum(jnp.where(pick, source, 0.0), axis=1, keepdims=True)
                here = jnp.where(iota((full, WIDTH), 1) == depth, column, matrix)
                straight[...] = here.astype(BF16)
                turned = dot_last(unit, matrix.astype(BF16))
                back[:, 0:full] = turned[0 : DEEP[depth]].astype(BF16)
        expand, shrink = weights[14][layer], weights[16][layer]
        keep.expand_back[layer] = dot_last(eye(HIDDEN, HIDDEN).astype(BF16), expand).astype(BF16)
        keep.shrink_back[layer] = dot_last(unit, shrink).astype(BF16)


def rows_in(start, stop, size):
    return [(at, min(at + size, stop)) for at in range(start, stop, size)]


def store_with_ones(ref, value, length):
    for at, end in rows_in(0, length, 16):
        piece = value[at : min(at + 16, value.shape[0])]
        if length == 12:
            row = iota(piece.shape, 0)
            piece = jnp.where(row < 12, piece, jnp.where(row == 12, 1.0, 0.0))
        elif end - at < 16:
            tail = (iota((8, piece.shape[1]), 0) == 0).astype(F32)
            piece = jnp.concatenate([piece, tail], axis=0)
        ref[at : at + 16, :] = piece.astype(BF16)


def padded(value, length):
    if length == 24:
        return jnp.concatenate([value, jnp.zeros((8, value.shape[1]), F32)], axis=0).astype(BF16)
    return value.astype(BF16)


def scale_rows(scale):
    return STARTS[scale], STARTS[scale] + ROWS_OF[LENGTHS[scale]]


def time_forward(layer, keep, lanes):
    if layer == 0:
        mean = keep.means[0]
        trend = dot(mean, keep.split[0:ROWS, lanes]) + dot(mean, keep.split[ROWS:, lanes])
    else:
        trend = dot(keep.means[0], keep.second_in[:, lanes])
    season_ref, trend_ref = keep.season, keep.trend
    source_ref, active_ref = keep.source, keep.active
    for at, end in rows_in(0, ROWS, 16):
        average = trend[at:end] * (1.0 / KERNEL)
        if layer == 0:
            value = keep.first_in[at:end, lanes]
        else:
            value = keep.second_in[at:end, lanes].astype(F32)
        trend_ref[at:end, lanes] = average
        season_ref[at:end, lanes] = value - average
    yield

    def block_forward(block, value_ref, from_scale, to_scale):
        into, to = FROM[block], TO[block]
        rows = ROWS_OF[to]
        at, end = scale_rows(from_scale)
        source = source_ref.at[layer, SOURCE_AT[block] : SOURCE_AT[block] + AUG[into], lanes]
        store_with_ones(source, value_ref[at:end, lanes], into)
        before = dot(
            keep.enter[layer, TO_AT[block] : TO_AT[block] + rows, 0 : AUG[into]], source[...]
        )
        yield
        active = active_ref.at[layer, ACTIVE_AT[block] : ACTIVE_AT[block] + AUG[to], lanes]
        for at, end in rows_in(0, rows, 16):
            value, slope = gelu_and_slope(before[at:end])
            keep.slope[layer, SLOPE_AT[block] + at : SLOPE_AT[block] + end, lanes] = slope
            if to >= 48:
                active[at:end, :] = value.astype(BF16)
            elif to == 24:
                if end - at < 16:
                    tail = (iota((8, value.shape[1]), 0) == 0).astype(F32)
                    value = jnp.concatenate([value, tail], axis=0)
                active[at : at + 16, :] = value.astype(BF16)
            else:
                store_with_ones(active, value, to)
        out = dot(keep.leave[layer, TO_AT[block] : TO_AT[block] + rows, 0 : AUG[to]], active[...])
        yield
        start, _ = scale_rows(to_scale)
        for at, end in rows_in(0, rows, 16):
            value_ref[start + at : start + end, lanes] += out[at:end]

    for step in range(3):
        pair = [
            block_forward(step, season_ref, step, step + 1),
            block_forward(3 + step, trend_ref, 3 - step, 2 - step),
        ]
        yield from alternate(pair)
    for at, end in rows_in(0, ROWS, 16):
        joined = season_ref[at:end, lanes] + trend_ref[at:end, lanes]
        keep.joined[layer, at:end, lanes] = joined.astype(BF16)


def alternate(tasks):
    tasks = list(tasks)
    while tasks:
        for task in list(tasks):
            try:
                next(task)
            except StopIteration:
                tasks.remove(task)
        if tasks:
            yield


def run(*tasks):
    for _ in alternate(tasks):
        pass


def mixed_rows(item, first, last):
    start = item // GROUP * STEPS * GROUP + item % GROUP
    return pl.ds(start + GROUP * first, last - first, GROUP)


def lanes_of(item):
    return slice(item * WIDTH, (item + 1) * WIDTH)


def wide_of(item):
    return slice(item * HIDDEN, (item + 1) * HIDDEN)


def stacked(ref, lanes, items, *first):
    return jnp.concatenate([ref[first + (slice(None), lanes(i))] for i in items], axis=0)


def branch_forward(layer, weights, keep, items):
    before = dot(stacked(keep.joined, lanes_of, items, layer), weights.expand[layer])
    yield
    bias = weights.expand_bias[layer : layer + 1, :].astype(F32)
    for place, item in enumerate(items):
        for at, end in rows_in(0, ROWS, 32):
            piece = before[place * ROWS + at : place * ROWS + end]
            value, slope = gelu_and_slope(piece + bias)
            keep.hidden[layer, at:end, wide_of(item)] = value.astype(BF16)
            keep.hidden_slope[layer, at:end, wide_of(item)] = slope
            if end % 64 == 0:
                yield
    branch = dot(stacked(keep.hidden, wide_of, items, layer), weights.shrink[layer])
    yield
    bias = weights.shrink_bias[layer : layer + 1, :].astype(F32)
    for place, item in enumerate(items):
        lanes = lanes_of(item)
        for at, end, scale_at in PIECES:
            if layer == 0:
                value = keep.first_in[at:end, lanes]
            else:
                value = keep.second_in[at:end, lanes].astype(F32)
            residual = value + (branch[place * ROWS + at : place * ROWS + end] + bias)
            centred = residual - jnp.mean(residual, axis=-1, keepdims=True)
            scale = lax.rsqrt(jnp.mean(centred * centred, axis=-1, keepdims=True) + EPSILON)
            normed = centred * scale
            keep.normed[layer, at:end, lanes] = normed
            keep.scale[layer, at:end, lanes] = jnp.broadcast_to(scale, normed.shape)
            gain = weights.gain[layer, scale_at : scale_at + 1, :].astype(F32)
            value = normed * gain + weights.shift[layer, scale_at : scale_at + 1, :].astype(F32)
            if layer == 0:
                if end == ROWS:
                    value = jnp.where(iota(value.shape, 0) < STEPS - at, value, 0.0)
                if at == 144:
                    held = value
                elif at == 168:
                    value = jnp.concatenate([held, value], axis=0)
                    keep.second_in[144:end, lanes] = value.astype(BF16)
                else:
                    keep.second_in[at:end, lanes] = value.astype(BF16)
            else:
                last = min(end, STEPS)
                keep.output_mixed[mixed_rows(item, at, last), :] = value[: last - at]
        yield


def fold(value):
    return jnp.sum(value.reshape(value.shape[0] // 8, 8, value.shape[1]), axis=0)


def branch_backward(layer, weights, keep, items):
    for item in items:
        lanes = lanes_of(item)
        for at, end, scale_at in PIECES:
            upstream = keep.upstream[at:end, lanes]
            normed = keep.normed[layer, at:end, lanes]
            keep.vector[layer, 1 + scale_at] += fold(upstream * normed)
            keep.vector[layer, 5 + scale_at] += fold(upstream)
            graded = upstream * weights.gain[layer, scale_at : scale_at + 1, :].astype(F32)
            average = jnp.mean(graded, axis=-1, keepdims=True)
            along = jnp.mean(graded * normed, axis=-1, keepdims=True)
            residual = (graded - average - normed * along) * keep.scale[layer, at:end, lanes]
            keep.back_residual[at:end, lanes] = residual
            keep.vector[layer, 0] += fold(residual)
            if at == 144:
                held = residual
            elif at == 168:
                residual = jnp.concatenate([held, residual], axis=0)
                keep.back_low[144:end, lanes] = residual.astype(BF16)
            else:
                keep.back_low[at:end, lanes] = residual.astype(BF16)
        yield
    back = dot(stacked(keep.back_low, lanes_of, items), keep.shrink_back[layer])
    yield
    for place, item in enumerate(items):
        wide = wide_of(item)
        for at, end in rows_in(0, ROWS, 32):
            piece = back[place * ROWS + at : place * ROWS + end]
            value = piece * keep.hidden_slope[layer, at:end, wide]
            keep.hidden_bias[layer] += fold(value)
            keep.back_hidden[at:end, wide] = value.astype(BF16)
        yield
    back = dot(stacked(keep.back_hidden, wide_of, items), keep.expand_back[layer])
    yield
    for place, item in enumerate(items):
        keep.back_joined[:, lanes_of(item)] = back[place * ROWS : (place + 1) * ROWS]


def branch_sums(layer, keep, items):
    keep.grad_expand[layer] += dot_first(
        stacked(keep.joined, lanes_of, items, layer), stacked(keep.back_hidden, wide_of, items)
    )
    yield
    keep.grad_shrink[layer] += dot_first(
        stacked(keep.back_low, lanes_of, items), stacked(keep.hidden, wide_of, items, layer)
    )


def time_backward(layer, keep, lanes, items):
    season_ref, trend_ref = keep.season, keep.trend
    for at, end in rows_in(0, ROWS, 16):
        value = keep.back_joined[at:end, lanes]
        season_ref[at:end, lanes] = value
        trend_ref[at:end, lanes] = value

    def block_backward(block, value_ref, from_scale, to_scale):
        into, to = FROM[block], TO[block]
        rows, deep = ROWS_OF[to], DEEP[to]
        at, end = scale_rows(to_scale)
        low = padded(value_ref[at:end, lanes], to)
        back = dot(keep.leave_back[layer, TO_AT[block] : TO_AT[block] + rows, 0:deep], low)
        active = keep.active[layer, ACTIVE_AT[block] : ACTIVE_AT[block] + AUG[to], lanes]
        keep.grad_leave[layer, block, 0:deep, 0 : AUG[to]] += dot_last(low, active)
        yield
        slope_at = SLOPE_AT[block]
        back = [
            back[at:end] * keep.slope[layer, slope_at + at : slope_at + end, lanes]
            for at, end in rows_in(0, rows, 16)
        ]
        low = padded(jnp.concatenate(back, axis=0), to)
        at = FROM_AT[block]
        out = dot(keep.enter_back[layer, at : at + ROWS_OF[into], 0:deep], low)
        source = keep.source[layer, SOURCE_AT[block] : SOURCE_AT[block] + AUG[into], lanes]
        keep.grad_enter[layer, block, 0:deep, 0 : AUG[into]] += dot_last(low, source)
        yield
        start, _ = scale_rows(from_scale)
        for at, end in rows_in(0, ROWS_OF[into], 16):
            value_ref[start + at : start + end, lanes] += out[at:end]

    for step in range(3):
        pair = [
            block_backward(2 - step, season_ref, 2 - step, 3 - step),
            block_backward(5 - step, trend_ref, step + 1, step),
        ]
        yield from alternate(pair)
    for at, end in rows_in(0, ROWS, 16):
        value = trend_ref[at:end, lanes] - season_ref[at:end, lanes]
        keep.difference[at:end, lanes] = value.astype(BF16)
    averaged = dot(keep.means[1], keep.difference[:, lanes])
    yield
    for at, end in rows_in(0, ROWS, 16):
        value = keep.back_residual[at:end, lanes] + season_ref[at:end, lanes]
        value = value + averaged[at:end] * (1.0 / KERNEL)
        if layer == 1:
            keep.upstream[at:end, lanes] = value.astype(BF16).astype(F32)
        else:
            end = min(end, STEPS)
            for place, item in enumerate(items):
                target = mixed_rows(item, at, end)
                keep.back_mixed[target, :] = value[: end - at, lanes_of(place)]


def pack(keep, packed_ref):
    for layer in range(LAYERS):
        enter = [keep.grad_enter[layer, block] for block in range(6)]
        leave = [keep.grad_leave[layer, block] for block in range(6)]

        def moved(value, lanes):
            return pltpu.roll(value, lanes, 1)

        packed_ref[layer, 0:48, :] = enter[0][0:48]
        packed_ref[layer, 48:144, :] = leave[5][0:96]
        packed_ref[layer, 144:192, :] = leave[0][0:48] + moved(leave[4][0:48], 64)
        first = enter[5][0:48] + moved(enter[4][0:48], 64)
        narrow = jnp.concatenate(
            [
                moved(enter[2][0:16], 96),
                moved(leave[2][0:16], 96),
                jnp.zeros((16, WIDTH), F32),
            ],
            axis=0,
        )
        corner = jnp.concatenate(
            [
                jnp.zeros((16, WIDTH), F32),
                moved(enter[3][0:24], 112),
                jnp.zeros((8, WIDTH), F32),
            ],
            axis=0,
        )
        packed_ref[layer, 192:240, :] = first + narrow + corner
        packed_ref[layer, 240:264, :] = enter[5][48:72] + moved(enter[1][0:24], 64)
        packed_ref[layer, 264:288, :] = (
            enter[5][72:96] + moved(leave[1][0:24], 64) + moved(leave[3][0:24], 96)
        )
        vector = jnp.sum(keep.vector[layer], axis=1)
        hidden_bias = jnp.sum(keep.hidden_bias[layer], axis=0, keepdims=True)
        packed_ref[layer, VECTORS_AT:EXPAND_AT, :] = jnp.concatenate(
            [
                vector,
                hidden_bias[:, 0:WIDTH],
                hidden_bias[:, WIDTH:],
                jnp.zeros((5, WIDTH), F32),
            ],
            axis=0,
        )
        for side in range(2):
            lanes = slice(side * WIDTH, (side + 1) * WIDTH)
            at = EXPAND_AT + side * WIDTH
            packed_ref[layer, at : at + WIDTH, :] = keep.grad_expand[layer, :, lanes]
            at = SHRINK_AT + side * WIDTH
            packed_ref[layer, at : at + WIDTH, :] = keep.grad_shrink[layer, :, lanes]


CONSTANT = ("counts",)
SHARED = dict(expand=14, expand_bias=15, shrink=16, shrink_bias=17, gain=18, shift=19)
PREPARED = dict(
    means=((2, ROWS, ROWS), BF16),
    enter=((LAYERS, TO_ROWS, WIDTH), BF16),
    leave=((LAYERS, TO_ROWS, WIDTH), BF16),
    enter_back=((LAYERS, FROM_ROWS, WIDTH), BF16),
    leave_back=((LAYERS, TO_ROWS, WIDTH), BF16),
    expand_back=((LAYERS, HIDDEN, WIDTH), BF16),
    shrink_back=((LAYERS, WIDTH, HIDDEN), BF16),
)
MICROS = 2
CUT = 36
ITEMS = MICROS * GROUP
LANES = ITEMS * WIDTH
WORK = dict(
    split=((2 * ROWS, LANES), BF16),
    first_in=((ROWS, LANES), F32),
    second_in=((ROWS, LANES), BF16),
    season=((ROWS, LANES), F32),
    trend=((ROWS, LANES), F32),
    source=((LAYERS, SOURCE_ROWS, LANES), BF16),
    active=((LAYERS, ACTIVE_ROWS, LANES), BF16),
    slope=((LAYERS, SLOPE_ROWS, LANES), F32),
    joined=((LAYERS, ROWS, LANES), BF16),
    hidden=((LAYERS, ROWS, 2 * LANES), BF16),
    hidden_slope=((LAYERS, ROWS, 2 * LANES), F32),
    normed=((LAYERS, ROWS, LANES), F32),
    scale=((LAYERS, ROWS, LANES), F32),
    upstream=((ROWS, LANES), F32),
    back_residual=((ROWS, LANES), F32),
    back_low=((ROWS, LANES), BF16),
    back_hidden=((ROWS, 2 * LANES), BF16),
    back_joined=((ROWS, LANES), F32),
    difference=((ROWS, LANES), BF16),
    output_mixed=((STEPS * ITEMS, WIDTH), F32),
    back_mixed=((STEPS * ITEMS, WIDTH), F32),
    packed=((LAYERS, USED_ROWS, WIDTH), F32),
)
SUMS = dict(
    grad_enter=((LAYERS, 6, 96, WIDTH), F32),
    grad_leave=((LAYERS, 6, 96, WIDTH), F32),
    grad_expand=((LAYERS, WIDTH, HIDDEN), F32),
    grad_shrink=((LAYERS, WIDTH, HIDDEN), F32),
    vector=((LAYERS, 9, 8, WIDTH), F32),
    hidden_bias=((LAYERS, 8, HIDDEN), F32),
)
UNREAD = pl.BlockSpec(memory_space=pl.ANY)
STAGE = dict(stage=((LAYERS, 6, 2, 96, WIDTH), F32))


class Keep:
    def add(self, names, refs):
        for name, ref in zip(names, refs):
            setattr(self, name, ref)
        return refs[len(names) :]


def narrowed(source, micro, step, target):
    first = (micro * STEPS + step) * GROUP
    for at, end in rows_in(0, target.shape[0], 96):
        target[at:end, :] = source[first + at : first + end, :].astype(BF16)
        yield


def mixing_kernel(position_ref, input_ref, tangent_ref, *refs):
    keep, weights = Keep(), Keep()
    refs = keep.add(CONSTANT, refs)
    every, refs = refs[0:20], refs[20:]
    weights.add(SHARED, [every[at] for at in SHARED.values()])
    results, packed_ref, send_ref, refs = refs[0:3], refs[3], refs[4], refs[5:]
    refs = keep.add(SUMS, keep.add(WORK, keep.add(PREPARED, refs)))
    keep.add(STAGE, refs)
    prepare(every, keep)

    for name in SUMS:
        ref = getattr(keep, name)
        ref[...] = jnp.zeros(ref.shape, F32)
    tail = (iota((16, LANES), 0) == 0).astype(F32).astype(BF16)
    for layer in range(LAYERS):
        for block in range(6):
            for ref, at, length in (
                (keep.source, SOURCE_AT[block], FROM[block]),
                (keep.active, ACTIVE_AT[block], TO[block]),
            ):
                if length >= 48:
                    ref[layer, at + length : at + length + 16, :] = tail
    keep.first_in[176:ROWS, :] = jnp.zeros((16, LANES), F32)
    keep.upstream[176:ROWS, :] = jnp.zeros((16, LANES), F32)
    flat = input_ref.reshape(STEPS * ITEMS, WIDTH)
    for item in range(ITEMS):
        keep.first_in[0:STEPS, lanes_of(item)] = flat[mixed_rows(item, 0, STEPS), :]
    for at, end in rows_in(0, ROWS, 16):
        value = keep.first_in[at:end, :]
        high = value.astype(BF16)
        keep.split[at:end, :] = high
        keep.split[ROWS + at : ROWS + end, :] = (value - high.astype(F32)).astype(BF16)

    size = 4
    parts = [list(range(at, at + size)) for at in range(0, ITEMS, size)]

    def part_lanes(part):
        return slice(parts[part][0] * WIDTH, (parts[part][-1] + 1) * WIDTH)

    def mix(layer, part):
        return [time_forward(layer, keep, part_lanes(part))]

    def branch(layer, part):
        return [branch_forward(layer, weights, keep, parts[part])]

    def back_branch(layer, part):
        return [branch_backward(layer, weights, keep, parts[part])]

    def back_mix(layer, part):
        return [
            branch_sums(layer, keep, parts[part]),
            time_backward(layer, keep, part_lanes(part), parts[part]),
        ]

    stages = [(mix, 0), (branch, 0), (mix, 1), (branch, 1)]
    stages += [(back_branch, 1), (back_mix, 1), (back_branch, 0), (back_mix, 0)]
    flat = tangent_ref.reshape(STEPS * ITEMS, WIDTH)
    for item in range(ITEMS):
        keep.upstream[0:STEPS, lanes_of(item)] = flat[mixed_rows(item, 0, STEPS), :]
    places = tuple(enumerate(((0, 0), (1, 0), (1, CUT))))
    for turn in range(len(stages) + 1):
        tasks = []
        for part in range(len(parts)):
            if 0 <= turn - part % 2 < len(stages):
                stage, layer = stages[turn - part % 2]
                tasks += stage(layer, part)
        if turn == 5:
            tasks += [narrowed(keep.output_mixed, *place, results[i].at[0]) for i, place in places]
        run(*tasks)
    run(*(narrowed(keep.back_mixed, *place, results[i].at[1]) for i, place in places))

    pack(keep, keep.packed)
    core = jnp.bitwise_and(position_ref[0], 1)
    for at, end in rows_in(0, USED_ROWS, 16):
        for side, ref in enumerate((packed_ref, send_ref)):
            value = jnp.where(core == side, keep.packed[0, at:end], keep.packed[1, at:end])
            ref[at:end, :] = value.astype(BF16)


def whole(array):
    zeros = (0,) * len(array.shape)
    return pl.BlockSpec(array.shape, lambda *_: zeros, pipeline_mode=pl.Buffered(1))


def mixing(position, series_input, cotangent, weights, rows):
    shape = jax.ShapeDtypeStruct
    data = pl.BlockSpec(
        (MICROS, STEPS, GROUP, WIDTH),
        lambda _, at: (0, 0, at[0], 0),
        pipeline_mode=pl.Buffered(1),
    )
    average = moving_average()
    inputs = [jnp.asarray(np.stack([average, average.T])), *weights]
    lengths = (STEPS, CUT, STEPS - CUT)
    outs = [shape((2, steps * GROUP, WIDTH), BF16) for steps in lengths]
    outs += [shape((rows, WIDTH), BF16)] * 2
    scratch = [*PREPARED.values(), *WORK.values(), *SUMS.values(), *STAGE.values()]
    return pl.pallas_call(
        mixing_kernel,
        out_shape=tuple(outs),
        grid_spec=pltpu.PrefetchScalarGridSpec(
            num_scalar_prefetch=1,
            grid=(1,),
            in_specs=[data, data] + [whole(i) for i in inputs],
            out_specs=tuple(whole(o) for o in outs),
            scratch_shapes=[pltpu.VMEM(*spec) for spec in scratch],
        ),
        compiler_params=pltpu.CompilerParams(
            dimension_semantics=("arbitrary",), vmem_limit_bytes=61 * 2**20
        ),
        cost_estimate=pl.CostEstimate(
            flops=20_000_000_000, bytes_accessed=4_000_000, transcendentals=0
        ),
        name="mixing",
    )(position, series_input, cotangent, *inputs)


def unpack_kernel(position_ref, own_ref, other_ref, *outs):
    core = jnp.bitwise_and(position_ref[0], 1)
    own = own_ref[...].astype(F32).reshape(-1, WIDTH)
    other = other_ref[...].astype(F32).reshape(-1, WIDTH)

    def row_of(value, lane, at, lanes):
        column = value[:, lane : lane + 1]
        rows = value.shape[0]
        pick = iota((rows, lanes), 1) - at == iota((rows, lanes), 0)
        return jnp.sum(jnp.where(pick, column, 0.0), axis=0, keepdims=True)

    for layer in range(LAYERS):
        slab = jnp.where(core == layer, own, other)

        def back(rows, lanes):
            value = slab[rows]
            return pltpu.roll(value, WIDTH - lanes, 1) if lanes else value

        enter = [
            slab[0:48],
            back(slice(240, 264), 64),
            back(slice(192, 208), 96),
            back(slice(208, 232), 112),
            back(slice(192, 240), 64),
            slab[192:288],
        ]
        leave = [
            slab[144:192],
            back(slice(264, 288), 64),
            back(slice(208, 224), 96),
            back(slice(264, 288), 96),
            back(slice(144, 192), 64),
            slab[48:144],
        ]
        for block in range(6):
            rows, cols = TO[block], FROM[block]
            for arg, value, depth in (
                (ENTER_ARG[block], enter[block], cols),
                (LEAVE_ARG[block], leave[block], rows),
            ):
                value = value[0 : ROWS_OF[rows]]
                if arg in TURNED:
                    value = value.T[0:depth, 0:rows]
                else:
                    value = value[0:rows, 0:depth]
                if arg in MIDDLE:
                    outs[arg][:, layer, :] = value
                else:
                    outs[arg][layer] = value
        for blocks in ((0, 1, 2), (3, 4, 5)):
            target = outs[BIAS_ARG[blocks[0]]]
            lanes = target.shape[2]
            first = jnp.zeros((1, lanes), F32)
            second = jnp.zeros((1, lanes), F32)
            for block in blocks:
                rows = TO[block]
                first = first + row_of(enter[block][0:rows], FROM[block], BIAS_AT[block], lanes)
                second = second + row_of(leave[block][0:rows], TO[block], BIAS_AT[block], lanes)
            target[layer, 0:1, :] = first
            target[layer, 1:2, :] = second
        for side in range(2):
            lanes = slice(side * WIDTH, (side + 1) * WIDTH)
            at = EXPAND_AT + side * WIDTH
            outs[14][layer, :, lanes] = slab[at : at + WIDTH]
            at = SHRINK_AT + side * WIDTH
            outs[16][layer, lanes, :] = slab[at : at + WIDTH].T
        vector = slab[VECTORS_AT:EXPAND_AT]
        outs[17][layer : layer + 1, :] = vector[0:1]
        outs[18][layer] = vector[1:5]
        outs[19][layer] = vector[5:9]
        outs[15][layer : layer + 1, 0:WIDTH] = vector[9:10]
        outs[15][layer : layer + 1, WIDTH:] = vector[10:11]


def local_call(kernel, scalars, arrays, shapes, name, after=()):
    unread = [UNREAD] * len(after)
    return pl.pallas_call(
        kernel,
        out_shape=shapes,
        grid_spec=pltpu.PrefetchScalarGridSpec(
            num_scalar_prefetch=len(scalars),
            grid=(1,),
            in_specs=[whole(a) for a in arrays] + unread,
            out_specs=tuple(whole(s) for s in shapes),
        ),
        compiler_params=pltpu.CompilerParams(vmem_limit_bytes=16 * 2**20),
        name=name,
    )(*scalars, *arrays, *after)


def join_kernel(*refs):
    out_ref = refs[-1]
    rows = out_ref.shape[1]
    for part in range(out_ref.shape[0]):
        at = slice(part * rows, (part + 1) * rows)
        total = refs[0][at, :].astype(F32)
        for ref in refs[1:-1]:
            total = total + ref[at, :].astype(F32)
        out_ref[part] = total.astype(BF16)


def total_kernel(count, *refs):
    total = 0.0
    for ref in refs[0:count]:
        for part in range(ref.shape[0]):
            total = total + ref[part].astype(F32)
    total = total.astype(BF16)
    for part in range(refs[-1].shape[0]):
        refs[-1][part] = total


def added(parts, shape, after=()):
    kernel = functools.partial(total_kernel, len(parts))
    return local_call(kernel, (), parts, (shape,), "total", after)[0]


def hold_kernel(value_ref, after_ref, out_ref):
    pass


def hold(value, after):
    return pl.pallas_call(
        hold_kernel,
        out_shape=jax.ShapeDtypeStruct(value.shape, value.dtype),
        in_specs=[UNREAD, UNREAD],
        out_specs=UNREAD,
        input_output_aliases={0: 0},
        compiler_params=pltpu.CompilerParams(vmem_limit_bytes=16 * 2**20),
        name="hold",
    )(value, after)


def exchanged(value, axis):
    return lax.ppermute(value, axis, [(0, 1), (1, 0)])


def swapped(parts):
    return lax.all_to_all(parts, "dp", 0, 0, tiled=True)


def widen_kernel(position_ref, own_ref, other_ref, *refs):
    outs = refs[-3:-1]
    refs[-1][...] = jnp.zeros(refs[-1].shape, F32)
    core = jnp.bitwise_and(position_ref[0], 1)
    for kind in range(2):
        for turn, ref in enumerate((own_ref, other_ref)):
            at = pl.multiple_of(jnp.bitwise_xor(core, turn) * GROUP, GROUP)
            value = ref[kind].astype(F32).reshape(-1, GROUP, WIDTH)
            outs[kind][0, :, pl.ds(at, GROUP), :] = value


def widen(position, turn, micro, micros, start, parts, before=(), after=()):
    series = 2 * GROUP
    cut = parts[0].shape[1] // (CUT * GROUP)

    def chip(at):
        return jnp.bitwise_xor(jnp.right_shift(at[0], 1), turn)

    piece = pl.BlockSpec((2, CUT * GROUP, WIDTH), lambda t, at: (0, t, 0))
    out = pl.BlockSpec(
        (1, CUT, series, WIDTH), lambda t, at: (micro, start // CUT + t, chip(at), 0)
    )
    shape = jax.ShapeDtypeStruct((micros, STEPS, 2 * series, WIDTH), F32)
    token = jax.ShapeDtypeStruct((GROUP, WIDTH), F32)
    return pl.pallas_call(
        widen_kernel,
        out_shape=(shape, shape, token),
        grid_spec=pltpu.PrefetchScalarGridSpec(
            num_scalar_prefetch=1,
            grid=(cut,),
            in_specs=[piece] * 2 + [UNREAD] * (len(before) + len(after)),
            out_specs=(out, out, whole(token)),
        ),
        input_output_aliases={3: 0, 4: 1} if before else {},
        compiler_params=pltpu.CompilerParams(vmem_limit_bytes=16 * 2**20),
        name="widen",
    )(position, *parts, *before, *after)


def shards(series_input, cotangent, *weights):
    micros = series_input.shape[0]
    across, core = lax.axis_index("x"), lax.axis_index("core")
    position = (across * 2 + core).astype(jnp.int32).reshape(1)
    views = [jnp.transpose(w, ORDER[i]) if i in ORDER else w for i, w in enumerate(weights)]
    share = 8 * lax.axis_size("dp")
    rows = -(-USED_ROWS // share) * share
    first, early, late, packed, send = mixing(position, series_input, cotangent, views, rows)

    devices = lax.axis_size("dp")
    part = jax.ShapeDtypeStruct((1, rows // devices, WIDTH), BF16)
    parts = jax.ShapeDtypeStruct((devices, rows // devices, WIDTH), BF16)
    there = exchanged(first, "x")
    near = (first, exchanged(first, "core"))
    other = exchanged(send, "core")
    (sent,) = local_call(join_kernel, (), (packed, other), (parts,), "join")
    *outs, token = widen(position, 0, 0, micros, 0, near, (), (sent,))
    across = exchanged(early, "x")
    near = (early, exchanged(early, "core"))
    total = added((swapped(sent),), part, (token, across))
    summed = exchanged(total, "x")
    sent = added((total, summed), parts)

    late, held = hold(late, sent), hold(there, sent)
    there = exchanged(late, "x")
    far = (held, exchanged(held, "core"))
    *outs, token = widen(position, 1, 0, micros, 0, far, outs, (sent,))
    *outs, token = widen(position, 0, 1, micros, 0, near, outs, (sent,))
    held = hold(across, sent)
    far = (held, exchanged(held, "core"))
    *outs, token = widen(position, 1, 1, micros, 0, far, outs, (sent,))
    near = (late, exchanged(late, "core"))
    *outs, token = widen(position, 0, 1, micros, CUT, near, outs, (sent,))
    total = hold(swapped(sent), token)
    other = exchanged(total, "core")
    held = hold(there, other)
    far = (held, exchanged(held, "core"))
    *outs, token = widen(position, 1, 1, micros, CUT, far, outs)
    shapes = tuple(jax.ShapeDtypeStruct(v.shape, F32) for v in views)
    grads = local_call(unpack_kernel, (position,), (total, other), shapes, "unpack")
    turned = {i: tuple(order.index(d) for d in range(3)) for i, order in ORDER.items()}
    grads = [jnp.transpose(g, turned[i]) if i in turned else g for i, g in enumerate(grads)]
    return tuple(outs) + tuple(grads)


def solution(mesh):
    dp = mesh.shape["dp"]
    mesh = jax.sharding.Mesh(mesh.devices.reshape(dp, 2, 2), ("dp", "x", "core"))
    data = P(None, None, "dp", None)
    return jax.shard_map(
        shards,
        mesh=mesh,
        in_specs=(data, data) + (P(),) * 20,
        out_specs=(data, data) + (P(),) * 20,
        check_vma=False,
    )
```

```python
import functools

import jax
import jax.numpy as jnp
import numpy as np
from jax import lax
from jax.experimental import pallas as pl
from jax.experimental.pallas import tpu as pltpu
from jax.sharding import PartitionSpec as P

F32 = jnp.float32
BF16 = jnp.bfloat16

LENGTHS = (96, 48, 24, 12)
STARTS = (0, 96, 144, 168)
STEPS = 180
ROWS = 192
KERNEL = 25
LAYERS = 2
WIDTH = 128
HIDDEN = 256
GROUP = 8
EPSILON = 1e-05

ROWS_OF = {96: 96, 48: 48, 24: 24, 12: 16}
AUG = {96: 112, 48: 64, 24: 32, 12: 16}
DEEP = {96: 96, 48: 48, 24: 32, 12: 16}

FROM = (96, 48, 24, 12, 24, 48)
TO = (48, 24, 12, 24, 48, 96)
BIAS_AT = (0, 48, 72, 144, 96, 0)
ENTER_ARG = (0, 1, 2, 9, 8, 7)
LEAVE_ARG = (3, 4, 5, 12, 11, 10)
BIAS_ARG = (6, 6, 6, 13, 13, 13)

ORDER = {2: (1, 0, 2), 5: (1, 0, 2), 7: (0, 2, 1), 8: (0, 2, 1), 9: (2, 0, 1)}
MIDDLE = (2, 5, 9)
TURNED = (7, 8, 9)


def offsets(sizes):
    total, found = 0, []
    for size in sizes:
        found.append(total)
        total += size
    return found, total


SOURCE_AT, SOURCE_ROWS = offsets([AUG[n] for n in FROM])
ACTIVE_AT, ACTIVE_ROWS = offsets([AUG[n] for n in TO])
SLOPE_AT, SLOPE_ROWS = offsets([ROWS_OF[n] for n in TO])
FROM_AT, FROM_ROWS = offsets([DEEP[n] for n in FROM])
TO_AT, TO_ROWS = offsets([DEEP[n] for n in TO])

PIECES = ((0, 48, 0), (48, 96, 0), (96, 144, 1), (144, 168, 2), (168, 192, 3))

VECTORS_AT = 288
EXPAND_AT = 304
SHRINK_AT = 560
USED_ROWS = 816

GELU_A = 0.7978845608028654
GELU_B = GELU_A * 0.044715


def dot(left, right):
    return lax.dot_general(left, right, (((1,), (0,)), ((), ())), preferred_element_type=F32)


def dot_last(left, right):
    return lax.dot_general(left, right, (((1,), (1,)), ((), ())), preferred_element_type=F32)


def dot_first(left, right):
    return lax.dot_general(left, right, (((0,), (0,)), ((), ())), preferred_element_type=F32)


def gelu_and_slope(u):
    square = u * u
    half = jnp.tanh(u * (GELU_A + GELU_B * square)) * 0.5 + 0.5
    value = u * half
    slope = half + (value - value * half) * (2.0 * GELU_A + 6.0 * GELU_B * square)
    return value, slope


def iota(shape, dim):
    return lax.broadcasted_iota(jnp.int32, shape, dim)


def eye(rows, lanes):
    return (iota((rows, lanes), 0) == iota((rows, lanes), 1)).astype(F32)


def moving_average():
    total = np.zeros((ROWS, ROWS), np.float32)
    for start, length in zip(STARTS, LENGTHS):
        for row in range(length):
            for offset in range(KERNEL):
                reached = min(max(row + offset - KERNEL // 2, 0), length - 1)
                total[start + row, start + reached] += 1.0
    return total


def prepare(weights, keep):
    keep.means[...] = keep.counts[...].astype(BF16)
    keep.stage[...] = jnp.zeros(keep.stage.shape, F32)
    unit = eye(WIDTH, WIDTH).astype(BF16)
    for layer in range(LAYERS):
        for block in range(6):
            rows, cols = TO[block], FROM[block]
            full = DEEP[rows]
            enter_back = keep.enter_back.at[layer, FROM_AT[block] : FROM_AT[block] + DEEP[cols]]
            near = slice(TO_AT[block], TO_AT[block] + full)
            leave_back = keep.leave_back.at[layer, near]
            for arg, depth, place, straight, back in (
                (ENTER_ARG[block], cols, 0, keep.enter.at[layer, near], enter_back),
                (LEAVE_ARG[block], rows, 1, keep.leave.at[layer, near], leave_back),
            ):
                stage = keep.stage.at[layer, block, place]
                if arg in MIDDLE:
                    value = weights[arg][...].astype(F32)[:, layer, :]
                else:
                    value = weights[arg][layer].astype(F32)
                stage[0 : value.shape[0], 0 : value.shape[1]] = value
                if arg in TURNED:
                    turned = dot_last(unit, stage[...].astype(BF16))
                    stage[:, 0:96] = turned[0:96]
                    stage[:, 96:] = jnp.zeros((96, WIDTH - 96), F32)
                matrix = stage[0:full, :]
                source = weights[BIAS_ARG[block]][layer, place : place + 1, :].astype(F32)
                at = BIAS_AT[block]
                lanes = source.shape[1]
                pick = iota((full, lanes), 1) - at == iota((full, lanes), 0)
                pick = pick & (iota((full, lanes), 0) < rows)
                column = jnp.sum(jnp.where(pick, source, 0.0), axis=1, keepdims=True)
                here = jnp.where(iota((full, WIDTH), 1) == depth, column, matrix)
                straight[...] = here.astype(BF16)
                turned = dot_last(unit, matrix.astype(BF16))
                back[:, 0:full] = turned[0 : DEEP[depth]].astype(BF16)
        expand, shrink = weights[14][layer], weights[16][layer]
        keep.expand_back[layer] = dot_last(eye(HIDDEN, HIDDEN).astype(BF16), expand).astype(BF16)
        keep.shrink_back[layer] = dot_last(unit, shrink).astype(BF16)


def rows_in(start, stop, size):
    return [(at, min(at + size, stop)) for at in range(start, stop, size)]


def store_with_ones(ref, value, length):
    for at, end in rows_in(0, length, 16):
        piece = value[at : min(at + 16, value.shape[0])]
        if length == 12:
            row = iota(piece.shape, 0)
            piece = jnp.where(row < 12, piece, jnp.where(row == 12, 1.0, 0.0))
        elif end - at < 16:
            tail = (iota((8, piece.shape[1]), 0) == 0).astype(F32)
            piece = jnp.concatenate([piece, tail], axis=0)
        ref[at : at + 16, :] = piece.astype(BF16)


def padded(value, length):
    if length == 24:
        return jnp.concatenate([value, jnp.zeros((8, value.shape[1]), F32)], axis=0).astype(BF16)
    return value.astype(BF16)


def scale_rows(scale):
    return STARTS[scale], STARTS[scale] + ROWS_OF[LENGTHS[scale]]


def time_forward(layer, keep, lanes):
    if layer == 0:
        mean = keep.means[0]
        trend = dot(mean, keep.split[0:ROWS, lanes]) + dot(mean, keep.split[ROWS:, lanes])
    else:
        trend = dot(keep.means[0], keep.second_in[:, lanes])
    season_ref, trend_ref = keep.season, keep.trend
    source_ref, active_ref = keep.source, keep.active
    for at, end in rows_in(0, ROWS, 16):
        average = trend[at:end] * (1.0 / KERNEL)
        if layer == 0:
            value = keep.first_in[at:end, lanes]
        else:
            value = keep.second_in[at:end, lanes].astype(F32)
        trend_ref[at:end, lanes] = average
        season_ref[at:end, lanes] = value - average
    yield

    def block_forward(block, value_ref, from_scale, to_scale):
        into, to = FROM[block], TO[block]
        rows = ROWS_OF[to]
        at, end = scale_rows(from_scale)
        source = source_ref.at[layer, SOURCE_AT[block] : SOURCE_AT[block] + AUG[into], lanes]
        store_with_ones(source, value_ref[at:end, lanes], into)
        before = dot(
            keep.enter[layer, TO_AT[block] : TO_AT[block] + rows, 0 : AUG[into]], source[...]
        )
        yield
        active = active_ref.at[layer, ACTIVE_AT[block] : ACTIVE_AT[block] + AUG[to], lanes]
        for at, end in rows_in(0, rows, 16):
            value, slope = gelu_and_slope(before[at:end])
            keep.slope[layer, SLOPE_AT[block] + at : SLOPE_AT[block] + end, lanes] = slope
            if to >= 48:
                active[at:end, :] = value.astype(BF16)
            elif to == 24:
                if end - at < 16:
                    tail = (iota((8, value.shape[1]), 0) == 0).astype(F32)
                    value = jnp.concatenate([value, tail], axis=0)
                active[at : at + 16, :] = value.astype(BF16)
            else:
                store_with_ones(active, value, to)
        out = dot(keep.leave[layer, TO_AT[block] : TO_AT[block] + rows, 0 : AUG[to]], active[...])
        yield
        start, _ = scale_rows(to_scale)
        for at, end in rows_in(0, rows, 16):
            value_ref[start + at : start + end, lanes] += out[at:end]

    for step in range(3):
        pair = [
            block_forward(step, season_ref, step, step + 1),
            block_forward(3 + step, trend_ref, 3 - step, 2 - step),
        ]
        yield from alternate(pair)
    for at, end in rows_in(0, ROWS, 16):
        joined = season_ref[at:end, lanes] + trend_ref[at:end, lanes]
        keep.joined[layer, at:end, lanes] = joined.astype(BF16)


def alternate(tasks):
    tasks = list(tasks)
    while tasks:
        for task in list(tasks):
            try:
                next(task)
            except StopIteration:
                tasks.remove(task)
        if tasks:
            yield


def run(*tasks):
    for _ in alternate(tasks):
        pass


def mixed_rows(item, first, last):
    start = item // GROUP * STEPS * GROUP + item % GROUP
    return pl.ds(start + GROUP * first, last - first, GROUP)


def lanes_of(item):
    return slice(item * WIDTH, (item + 1) * WIDTH)


def wide_of(item):
    return slice(item * HIDDEN, (item + 1) * HIDDEN)


def stacked(ref, lanes, items, *first):
    return jnp.concatenate([ref[first + (slice(None), lanes(i))] for i in items], axis=0)


def branch_forward(layer, weights, keep, items):
    before = dot(stacked(keep.joined, lanes_of, items, layer), weights.expand[layer])
    yield
    bias = weights.expand_bias[layer : layer + 1, :].astype(F32)
    for place, item in enumerate(items):
        for at, end in rows_in(0, ROWS, 32):
            piece = before[place * ROWS + at : place * ROWS + end]
            value, slope = gelu_and_slope(piece + bias)
            keep.hidden[layer, at:end, wide_of(item)] = value.astype(BF16)
            keep.hidden_slope[layer, at:end, wide_of(item)] = slope
            if end % 64 == 0:
                yield
    branch = dot(stacked(keep.hidden, wide_of, items, layer), weights.shrink[layer])
    yield
    bias = weights.shrink_bias[layer : layer + 1, :].astype(F32)
    for place, item in enumerate(items):
        lanes = lanes_of(item)
        for at, end, scale_at in PIECES:
            if layer == 0:
                value = keep.first_in[at:end, lanes]
            else:
                value = keep.second_in[at:end, lanes].astype(F32)
            residual = value + (branch[place * ROWS + at : place * ROWS + end] + bias)
            centred = residual - jnp.mean(residual, axis=-1, keepdims=True)
            scale = lax.rsqrt(jnp.mean(centred * centred, axis=-1, keepdims=True) + EPSILON)
            normed = centred * scale
            keep.normed[layer, at:end, lanes] = normed
            keep.scale[layer, at:end, lanes] = jnp.broadcast_to(scale, normed.shape)
            gain = weights.gain[layer, scale_at : scale_at + 1, :].astype(F32)
            value = normed * gain + weights.shift[layer, scale_at : scale_at + 1, :].astype(F32)
            if layer == 0:
                if end == ROWS:
                    value = jnp.where(iota(value.shape, 0) < STEPS - at, value, 0.0)
                if at == 144:
                    held = value
                elif at == 168:
                    value = jnp.concatenate([held, value], axis=0)
                    keep.second_in[144:end, lanes] = value.astype(BF16)
                else:
                    keep.second_in[at:end, lanes] = value.astype(BF16)
            else:
                last = min(end, STEPS)
                keep.output_mixed[mixed_rows(item, at, last), :] = value[: last - at]
        yield


def fold(value):
    return jnp.sum(value.reshape(value.shape[0] // 8, 8, value.shape[1]), axis=0)


def branch_backward(layer, weights, keep, items):
    for item in items:
        lanes = lanes_of(item)
        for at, end, scale_at in PIECES:
            upstream = keep.upstream[at:end, lanes]
            normed = keep.normed[layer, at:end, lanes]
            keep.vector[layer, 1 + scale_at] += fold(upstream * normed)
            keep.vector[layer, 5 + scale_at] += fold(upstream)
            graded = upstream * weights.gain[layer, scale_at : scale_at + 1, :].astype(F32)
            average = jnp.mean(graded, axis=-1, keepdims=True)
            along = jnp.mean(graded * normed, axis=-1, keepdims=True)
            residual = (graded - average - normed * along) * keep.scale[layer, at:end, lanes]
            keep.back_residual[at:end, lanes] = residual
            keep.vector[layer, 0] += fold(residual)
            if at == 144:
                held = residual
            elif at == 168:
                residual = jnp.concatenate([held, residual], axis=0)
                keep.back_low[144:end, lanes] = residual.astype(BF16)
            else:
                keep.back_low[at:end, lanes] = residual.astype(BF16)
        yield
    back = dot(stacked(keep.back_low, lanes_of, items), keep.shrink_back[layer])
    yield
    for place, item in enumerate(items):
        wide = wide_of(item)
        for at, end in rows_in(0, ROWS, 32):
            piece = back[place * ROWS + at : place * ROWS + end]
            value = piece * keep.hidden_slope[layer, at:end, wide]
            keep.hidden_bias[layer] += fold(value)
            keep.back_hidden[at:end, wide] = value.astype(BF16)
        yield
    back = dot(stacked(keep.back_hidden, wide_of, items), keep.expand_back[layer])
    yield
    for place, item in enumerate(items):
        keep.back_joined[:, lanes_of(item)] = back[place * ROWS : (place + 1) * ROWS]


def branch_sums(layer, keep, items):
    keep.grad_expand[layer] += dot_first(
        stacked(keep.joined, lanes_of, items, layer), stacked(keep.back_hidden, wide_of, items)
    )
    yield
    keep.grad_shrink[layer] += dot_first(
        stacked(keep.back_low, lanes_of, items), stacked(keep.hidden, wide_of, items, layer)
    )


def time_backward(layer, keep, lanes, items):
    season_ref, trend_ref = keep.season, keep.trend
    for at, end in rows_in(0, ROWS, 16):
        value = keep.back_joined[at:end, lanes]
        season_ref[at:end, lanes] = value
        trend_ref[at:end, lanes] = value

    def block_backward(block, value_ref, from_scale, to_scale):
        into, to = FROM[block], TO[block]
        rows, deep = ROWS_OF[to], DEEP[to]
        at, end = scale_rows(to_scale)
        low = padded(value_ref[at:end, lanes], to)
        back = dot(keep.leave_back[layer, TO_AT[block] : TO_AT[block] + rows, 0:deep], low)
        active = keep.active[layer, ACTIVE_AT[block] : ACTIVE_AT[block] + AUG[to], lanes]
        keep.grad_leave[layer, block, 0:deep, 0 : AUG[to]] += dot_last(low, active)
        yield
        slope_at = SLOPE_AT[block]
        back = [
            back[at:end] * keep.slope[layer, slope_at + at : slope_at + end, lanes]
            for at, end in rows_in(0, rows, 16)
        ]
        low = padded(jnp.concatenate(back, axis=0), to)
        at = FROM_AT[block]
        out = dot(keep.enter_back[layer, at : at + ROWS_OF[into], 0:deep], low)
        source = keep.source[layer, SOURCE_AT[block] : SOURCE_AT[block] + AUG[into], lanes]
        keep.grad_enter[layer, block, 0:deep, 0 : AUG[into]] += dot_last(low, source)
        yield
        start, _ = scale_rows(from_scale)
        for at, end in rows_in(0, ROWS_OF[into], 16):
            value_ref[start + at : start + end, lanes] += out[at:end]

    for step in range(3):
        pair = [
            block_backward(2 - step, season_ref, 2 - step, 3 - step),
            block_backward(5 - step, trend_ref, step + 1, step),
        ]
        yield from alternate(pair)
    for at, end in rows_in(0, ROWS, 16):
        value = trend_ref[at:end, lanes] - season_ref[at:end, lanes]
        keep.difference[at:end, lanes] = value.astype(BF16)
    averaged = dot(keep.means[1], keep.difference[:, lanes])
    yield
    for at, end in rows_in(0, ROWS, 16):
        value = keep.back_residual[at:end, lanes] + season_ref[at:end, lanes]
        value = value + averaged[at:end] * (1.0 / KERNEL)
        if layer == 1:
            keep.upstream[at:end, lanes] = value.astype(BF16).astype(F32)
        else:
            end = min(end, STEPS)
            for place, item in enumerate(items):
                target = mixed_rows(item, at, end)
                keep.back_mixed[target, :] = value[: end - at, lanes_of(place)]


def pack(keep, packed_ref):
    for layer in range(LAYERS):
        enter = [keep.grad_enter[layer, block] for block in range(6)]
        leave = [keep.grad_leave[layer, block] for block in range(6)]

        def moved(value, lanes):
            return pltpu.roll(value, lanes, 1)

        packed_ref[layer, 0:48, :] = enter[0][0:48]
        packed_ref[layer, 48:144, :] = leave[5][0:96]
        packed_ref[layer, 144:192, :] = leave[0][0:48] + moved(leave[4][0:48], 64)
        first = enter[5][0:48] + moved(enter[4][0:48], 64)
        narrow = jnp.concatenate(
            [
                moved(enter[2][0:16], 96),
                moved(leave[2][0:16], 96),
                jnp.zeros((16, WIDTH), F32),
            ],
            axis=0,
        )
        corner = jnp.concatenate(
            [
                jnp.zeros((16, WIDTH), F32),
                moved(enter[3][0:24], 112),
                jnp.zeros((8, WIDTH), F32),
            ],
            axis=0,
        )
        packed_ref[layer, 192:240, :] = first + narrow + corner
        packed_ref[layer, 240:264, :] = enter[5][48:72] + moved(enter[1][0:24], 64)
        packed_ref[layer, 264:288, :] = (
            enter[5][72:96] + moved(leave[1][0:24], 64) + moved(leave[3][0:24], 96)
        )
        vector = jnp.sum(keep.vector[layer], axis=1)
        hidden_bias = jnp.sum(keep.hidden_bias[layer], axis=0, keepdims=True)
        packed_ref[layer, VECTORS_AT:EXPAND_AT, :] = jnp.concatenate(
            [
                vector,
                hidden_bias[:, 0:WIDTH],
                hidden_bias[:, WIDTH:],
                jnp.zeros((5, WIDTH), F32),
            ],
            axis=0,
        )
        for side in range(2):
            lanes = slice(side * WIDTH, (side + 1) * WIDTH)
            at = EXPAND_AT + side * WIDTH
            packed_ref[layer, at : at + WIDTH, :] = keep.grad_expand[layer, :, lanes]
            at = SHRINK_AT + side * WIDTH
            packed_ref[layer, at : at + WIDTH, :] = keep.grad_shrink[layer, :, lanes]


CONSTANT = ("counts",)
SHARED = dict(expand=14, expand_bias=15, shrink=16, shrink_bias=17, gain=18, shift=19)
PREPARED = dict(
    means=((2, ROWS, ROWS), BF16),
    enter=((LAYERS, TO_ROWS, WIDTH), BF16),
    leave=((LAYERS, TO_ROWS, WIDTH), BF16),
    enter_back=((LAYERS, FROM_ROWS, WIDTH), BF16),
    leave_back=((LAYERS, TO_ROWS, WIDTH), BF16),
    expand_back=((LAYERS, HIDDEN, WIDTH), BF16),
    shrink_back=((LAYERS, WIDTH, HIDDEN), BF16),
)
MICROS = 2
ITEMS = MICROS * GROUP
LANES = ITEMS * WIDTH
WORK = dict(
    split=((2 * ROWS, LANES), BF16),
    first_in=((ROWS, LANES), F32),
    second_in=((ROWS, LANES), BF16),
    season=((ROWS, LANES), F32),
    trend=((ROWS, LANES), F32),
    source=((LAYERS, SOURCE_ROWS, LANES), BF16),
    active=((LAYERS, ACTIVE_ROWS, LANES), BF16),
    slope=((LAYERS, SLOPE_ROWS, LANES), F32),
    joined=((LAYERS, ROWS, LANES), BF16),
    hidden=((LAYERS, ROWS, 2 * LANES), BF16),
    hidden_slope=((LAYERS, ROWS, 2 * LANES), F32),
    normed=((LAYERS, ROWS, LANES), F32),
    scale=((LAYERS, ROWS, LANES), F32),
    upstream=((ROWS, LANES), F32),
    back_residual=((ROWS, LANES), F32),
    back_low=((ROWS, LANES), BF16),
    back_hidden=((ROWS, 2 * LANES), BF16),
    back_joined=((ROWS, LANES), F32),
    difference=((ROWS, LANES), BF16),
    output_mixed=((STEPS * ITEMS, WIDTH), F32),
    back_mixed=((STEPS * ITEMS, WIDTH), F32),
    packed=((LAYERS, USED_ROWS, WIDTH), F32),
)
SUMS = dict(
    grad_enter=((LAYERS, 6, 96, WIDTH), F32),
    grad_leave=((LAYERS, 6, 96, WIDTH), F32),
    grad_expand=((LAYERS, WIDTH, HIDDEN), F32),
    grad_shrink=((LAYERS, WIDTH, HIDDEN), F32),
    vector=((LAYERS, 9, 8, WIDTH), F32),
    hidden_bias=((LAYERS, 8, HIDDEN), F32),
)
UNREAD = pl.BlockSpec(memory_space=pl.ANY)
STAGE = dict(stage=((LAYERS, 6, 2, 96, WIDTH), F32))


class Keep:
    def add(self, names, refs):
        for name, ref in zip(names, refs):
            setattr(self, name, ref)
        return refs[len(names) :]


def narrowed(source, micro, target):
    first = micro * STEPS * GROUP
    for at, end in rows_in(0, STEPS * GROUP, 96):
        target[at:end, :] = source[first + at : first + end, :].astype(BF16)
        yield


def mixing_kernel(position_ref, input_ref, tangent_ref, *refs):
    keep, weights = Keep(), Keep()
    refs = keep.add(CONSTANT, refs)
    every, refs = refs[0:20], refs[20:]
    weights.add(SHARED, [every[at] for at in SHARED.values()])
    results, packed_ref, send_ref, refs = refs[0:MICROS], *refs[MICROS : MICROS + 2], refs[4:]
    refs = keep.add(SUMS, keep.add(WORK, keep.add(PREPARED, refs)))
    keep.add(STAGE, refs)
    prepare(every, keep)

    for name in SUMS:
        ref = getattr(keep, name)
        ref[...] = jnp.zeros(ref.shape, F32)
    tail = (iota((16, LANES), 0) == 0).astype(F32).astype(BF16)
    for layer in range(LAYERS):
        for block in range(6):
            for ref, at, length in (
                (keep.source, SOURCE_AT[block], FROM[block]),
                (keep.active, ACTIVE_AT[block], TO[block]),
            ):
                if length >= 48:
                    ref[layer, at + length : at + length + 16, :] = tail
    keep.first_in[176:ROWS, :] = jnp.zeros((16, LANES), F32)
    keep.upstream[176:ROWS, :] = jnp.zeros((16, LANES), F32)
    flat = input_ref.reshape(STEPS * ITEMS, WIDTH)
    for item in range(ITEMS):
        keep.first_in[0:STEPS, lanes_of(item)] = flat[mixed_rows(item, 0, STEPS), :]
    for at, end in rows_in(0, ROWS, 16):
        value = keep.first_in[at:end, :]
        high = value.astype(BF16)
        keep.split[at:end, :] = high
        keep.split[ROWS + at : ROWS + end, :] = (value - high.astype(F32)).astype(BF16)

    size = 4
    parts = [list(range(at, at + size)) for at in range(0, ITEMS, size)]

    def part_lanes(part):
        return slice(parts[part][0] * WIDTH, (parts[part][-1] + 1) * WIDTH)

    def mix(layer, part):
        return [time_forward(layer, keep, part_lanes(part))]

    def branch(layer, part):
        return [branch_forward(layer, weights, keep, parts[part])]

    def back_branch(layer, part):
        return [branch_backward(layer, weights, keep, parts[part])]

    def back_mix(layer, part):
        return [
            branch_sums(layer, keep, parts[part]),
            time_backward(layer, keep, part_lanes(part), parts[part]),
        ]

    stages = [(mix, 0), (branch, 0), (mix, 1), (branch, 1)]
    stages += [(back_branch, 1), (back_mix, 1), (back_branch, 0), (back_mix, 0)]
    flat = tangent_ref.reshape(STEPS * ITEMS, WIDTH)
    for item in range(ITEMS):
        keep.upstream[0:STEPS, lanes_of(item)] = flat[mixed_rows(item, 0, STEPS), :]
    for turn in range(len(stages) + 1):
        tasks = []
        for part in range(len(parts)):
            if 0 <= turn - part % 2 < len(stages):
                stage, layer = stages[turn - part % 2]
                tasks += stage(layer, part)
        if turn == 5:
            tasks += [narrowed(keep.output_mixed, m, results[m].at[0]) for m in range(MICROS)]
        run(*tasks)
    run(*(narrowed(keep.back_mixed, m, results[m].at[1]) for m in range(MICROS)))

    pack(keep, keep.packed)
    core = jnp.bitwise_and(position_ref[0], 1)
    for at, end in rows_in(0, USED_ROWS, 16):
        for side, ref in enumerate((packed_ref, send_ref)):
            value = jnp.where(core == side, keep.packed[0, at:end], keep.packed[1, at:end])
            ref[at:end, :] = value.astype(BF16)


def whole(array):
    zeros = (0,) * len(array.shape)
    return pl.BlockSpec(array.shape, lambda *_: zeros, pipeline_mode=pl.Buffered(1))


def mixing(position, series_input, cotangent, weights, rows):
    shape = jax.ShapeDtypeStruct
    data = pl.BlockSpec(
        (MICROS, STEPS, GROUP, WIDTH),
        lambda _, at: (0, 0, at[0], 0),
        pipeline_mode=pl.Buffered(1),
    )
    average = moving_average()
    inputs = [jnp.asarray(np.stack([average, average.T])), *weights]
    outs = [shape((2, STEPS * GROUP, WIDTH), BF16)] * MICROS + [shape((rows, WIDTH), BF16)] * 2
    scratch = [*PREPARED.values(), *WORK.values(), *SUMS.values(), *STAGE.values()]
    return pl.pallas_call(
        mixing_kernel,
        out_shape=tuple(outs),
        grid_spec=pltpu.PrefetchScalarGridSpec(
            num_scalar_prefetch=1,
            grid=(1,),
            in_specs=[data, data] + [whole(i) for i in inputs],
            out_specs=tuple(whole(o) for o in outs),
            scratch_shapes=[pltpu.VMEM(*spec) for spec in scratch],
        ),
        compiler_params=pltpu.CompilerParams(
            dimension_semantics=("arbitrary",), vmem_limit_bytes=61 * 2**20
        ),
        cost_estimate=pl.CostEstimate(
            flops=20_000_000_000, bytes_accessed=4_000_000, transcendentals=0
        ),
        name="mixing",
    )(position, series_input, cotangent, *inputs)


def unpack_kernel(position_ref, own_ref, other_ref, *outs):
    core = jnp.bitwise_and(position_ref[0], 1)
    own = own_ref[...].astype(F32).reshape(-1, WIDTH)
    other = other_ref[...].astype(F32).reshape(-1, WIDTH)

    def row_of(value, lane, at, lanes):
        column = value[:, lane : lane + 1]
        rows = value.shape[0]
        pick = iota((rows, lanes), 1) - at == iota((rows, lanes), 0)
        return jnp.sum(jnp.where(pick, column, 0.0), axis=0, keepdims=True)

    for layer in range(LAYERS):
        slab = jnp.where(core == layer, own, other)

        def back(rows, lanes):
            value = slab[rows]
            return pltpu.roll(value, WIDTH - lanes, 1) if lanes else value

        enter = [
            slab[0:48],
            back(slice(240, 264), 64),
            back(slice(192, 208), 96),
            back(slice(208, 232), 112),
            back(slice(192, 240), 64),
            slab[192:288],
        ]
        leave = [
            slab[144:192],
            back(slice(264, 288), 64),
            back(slice(208, 224), 96),
            back(slice(264, 288), 96),
            back(slice(144, 192), 64),
            slab[48:144],
        ]
        for block in range(6):
            rows, cols = TO[block], FROM[block]
            for arg, value, depth in (
                (ENTER_ARG[block], enter[block], cols),
                (LEAVE_ARG[block], leave[block], rows),
            ):
                value = value[0 : ROWS_OF[rows]]
                if arg in TURNED:
                    value = value.T[0:depth, 0:rows]
                else:
                    value = value[0:rows, 0:depth]
                if arg in MIDDLE:
                    outs[arg][:, layer, :] = value
                else:
                    outs[arg][layer] = value
        for blocks in ((0, 1, 2), (3, 4, 5)):
            target = outs[BIAS_ARG[blocks[0]]]
            lanes = target.shape[2]
            first = jnp.zeros((1, lanes), F32)
            second = jnp.zeros((1, lanes), F32)
            for block in blocks:
                rows = TO[block]
                first = first + row_of(enter[block][0:rows], FROM[block], BIAS_AT[block], lanes)
                second = second + row_of(leave[block][0:rows], TO[block], BIAS_AT[block], lanes)
            target[layer, 0:1, :] = first
            target[layer, 1:2, :] = second
        for side in range(2):
            lanes = slice(side * WIDTH, (side + 1) * WIDTH)
            at = EXPAND_AT + side * WIDTH
            outs[14][layer, :, lanes] = slab[at : at + WIDTH]
            at = SHRINK_AT + side * WIDTH
            outs[16][layer, lanes, :] = slab[at : at + WIDTH].T
        vector = slab[VECTORS_AT:EXPAND_AT]
        outs[17][layer : layer + 1, :] = vector[0:1]
        outs[18][layer] = vector[1:5]
        outs[19][layer] = vector[5:9]
        outs[15][layer : layer + 1, 0:WIDTH] = vector[9:10]
        outs[15][layer : layer + 1, WIDTH:] = vector[10:11]


def local_call(kernel, scalars, arrays, shapes, name, after=()):
    unread = [UNREAD] * len(after)
    return pl.pallas_call(
        kernel,
        out_shape=shapes,
        grid_spec=pltpu.PrefetchScalarGridSpec(
            num_scalar_prefetch=len(scalars),
            grid=(1,),
            in_specs=[whole(a) for a in arrays] + unread,
            out_specs=tuple(whole(s) for s in shapes),
        ),
        compiler_params=pltpu.CompilerParams(vmem_limit_bytes=16 * 2**20),
        name=name,
    )(*scalars, *arrays, *after)


def join_kernel(*refs):
    out_ref = refs[-1]
    rows = out_ref.shape[1]
    for part in range(out_ref.shape[0]):
        at = slice(part * rows, (part + 1) * rows)
        total = refs[0][at, :].astype(F32)
        for ref in refs[1:-1]:
            total = total + ref[at, :].astype(F32)
        out_ref[part] = total.astype(BF16)


def total_kernel(count, *refs):
    total = 0.0
    for ref in refs[0:count]:
        for part in range(ref.shape[0]):
            total = total + ref[part].astype(F32)
    total = total.astype(BF16)
    for part in range(refs[-1].shape[0]):
        refs[-1][part] = total


def added(parts, shape, after=()):
    kernel = functools.partial(total_kernel, len(parts))
    return local_call(kernel, (), parts, (shape,), "total", after)[0]


def hold_kernel(value_ref, after_ref, out_ref):
    pass


def hold(value, after):
    return pl.pallas_call(
        hold_kernel,
        out_shape=jax.ShapeDtypeStruct(value.shape, value.dtype),
        in_specs=[UNREAD, UNREAD],
        out_specs=UNREAD,
        input_output_aliases={0: 0},
        compiler_params=pltpu.CompilerParams(vmem_limit_bytes=16 * 2**20),
        name="hold",
    )(value, after)


def exchanged(value, axis):
    return lax.ppermute(value, axis, [(0, 1), (1, 0)])


def swapped(parts):
    return lax.all_to_all(parts, "dp", 0, 0, tiled=True)


def widen_kernel(position_ref, own_ref, other_ref, *refs):
    outs = refs[-3:-1]
    refs[-1][...] = jnp.zeros(refs[-1].shape, F32)
    core = jnp.bitwise_and(position_ref[0], 1)
    for kind in range(2):
        for turn, ref in enumerate((own_ref, other_ref)):
            at = pl.multiple_of(jnp.bitwise_xor(core, turn) * GROUP, GROUP)
            value = ref[kind].astype(F32).reshape(-1, GROUP, WIDTH)
            outs[kind][0, :, pl.ds(at, GROUP), :] = value


def widen(position, turn, micro, micros, parts, before=(), after=()):
    series = 2 * GROUP
    cut = 4

    def chip(at):
        return jnp.bitwise_xor(jnp.right_shift(at[0], 1), turn)

    piece = pl.BlockSpec((2, STEPS * GROUP // cut, WIDTH), lambda t, at: (0, t, 0))
    out = pl.BlockSpec((1, STEPS // cut, series, WIDTH), lambda t, at: (micro, t, chip(at), 0))
    shape = jax.ShapeDtypeStruct((micros, STEPS, 2 * series, WIDTH), F32)
    token = jax.ShapeDtypeStruct((GROUP, WIDTH), F32)
    return pl.pallas_call(
        widen_kernel,
        out_shape=(shape, shape, token),
        grid_spec=pltpu.PrefetchScalarGridSpec(
            num_scalar_prefetch=1,
            grid=(cut,),
            in_specs=[piece] * 2 + [UNREAD] * (len(before) + len(after)),
            out_specs=(out, out, whole(token)),
        ),
        input_output_aliases={3: 0, 4: 1} if before else {},
        compiler_params=pltpu.CompilerParams(vmem_limit_bytes=16 * 2**20),
        name="widen",
    )(position, *parts, *before, *after)


def shards(series_input, cotangent, *weights):
    micros = series_input.shape[0]
    across, core = lax.axis_index("x"), lax.axis_index("core")
    position = (across * 2 + core).astype(jnp.int32).reshape(1)
    views = [jnp.transpose(w, ORDER[i]) if i in ORDER else w for i, w in enumerate(weights)]
    share = 8 * lax.axis_size("dp")
    rows = -(-USED_ROWS // share) * share
    first, second, packed, send = mixing(position, series_input, cotangent, views, rows)

    devices = lax.axis_size("dp")
    part = jax.ShapeDtypeStruct((1, rows // devices, WIDTH), BF16)
    parts = jax.ShapeDtypeStruct((devices, rows // devices, WIDTH), BF16)
    there = exchanged(first, "x")
    near = (first, exchanged(first, "core"))
    other = exchanged(send, "core")
    (sent,) = local_call(join_kernel, (), (packed, other), (parts,), "join")
    *outs, token = widen(position, 0, 0, micros, near, (), (sent,))
    total = added((swapped(sent),), part, (token,))
    across = exchanged(total, "x")
    sent = added((total, across), parts)

    second, held = hold(second, sent), hold(there, sent)
    far = (held, exchanged(held, "core"))
    *outs, token = widen(position, 1, 0, micros, far, outs, (sent,))
    there = exchanged(second, "x")
    near = (second, exchanged(second, "core"))
    *outs, token = widen(position, 0, 1, micros, near, outs, (sent,))
    total = hold(swapped(sent), token)
    other = exchanged(total, "core")
    held = hold(there, other)
    far = (held, exchanged(held, "core"))
    *outs, token = widen(position, 1, 1, micros, far, outs)
    shapes = tuple(jax.ShapeDtypeStruct(v.shape, F32) for v in views)
    grads = local_call(unpack_kernel, (position,), (total, other), shapes, "unpack")
    turned = {i: tuple(order.index(d) for d in range(3)) for i, order in ORDER.items()}
    grads = [jnp.transpose(g, turned[i]) if i in turned else g for i, g in enumerate(grads)]
    return tuple(outs) + tuple(grads)


def solution(mesh):
    dp = mesh.shape["dp"]
    mesh = jax.sharding.Mesh(mesh.devices.reshape(dp, 2, 2), ("dp", "x", "core"))
    data = P(None, None, "dp", None)
    return jax.shard_map(
        shards,
        mesh=mesh,
        in_specs=(data, data) + (P(),) * 20,
        out_specs=(data, data) + (P(),) * 20,
        check_vma=False,
    )
```
